32 devices in a mesh: row: 8 (over z, y), col: 4 (over x, core).
Axes of the slice: x: 2, y: 2, z: 4, core: 2. Of those that a mesh axis runs over, the one named last changes fastest.
Arguments:
- leaf_basis: bfloat16 [64, 2048, 128], P(('row', 'col')), may hold values from -6 to 6
- transfer_leaf: float32 [64, 128, 128], P(('row', 'col')), may hold values from -0.5 to 0.5
- transfer_mid: float32 [32, 128, 128], P(('row', 'col')), may hold values from -0.5 to 0.5
- transfer_top: float32 [8, 2, 128, 128], P('row'), may hold values from -0.5 to 0.5
- coupling_leaf: bfloat16 [64, 112, 128, 128], P(('row', 'col')), may hold values from -6 to 6
- coupling_mid: bfloat16 [32, 112, 128, 128], P(('row', 'col')), may hold values from -6 to 6
- partners_leaf: int32 [64, 112], P(('row', 'col')), may hold values from 0 to 63, as said below
- partners_mid: int32 [32, 112], P(('row', 'col')), may hold values from 0 to 31, as said below
- counts_leaf: int32 [64], P(('row', 'col')), may hold values from 1 to 112, as said below
- counts_mid: int32 [32], P(('row', 'col')), may hold values from 1 to 112, as said below
- ranks: int32 [4], replicated, may hold values from 64 to 128
Outputs:
- leaf_q: bfloat16 [64, 2048, 128], P(('row', 'col'))
- transfer_leaf_out: float32 [64, 128, 128], P(('row', 'col'))
- transfer_mid_out: float32 [32, 128, 128], P(('row', 'col'))
- transfer_top_out: float32 [8, 4, 64, 128], P('row', 'col')
- coupling_leaf_out: bfloat16 [64, 112, 128, 128], P(('row', 'col'))
- coupling_mid_out: bfloat16 [32, 112, 128, 128], P(('row', 'col'))
The draws below stay inside these ranges and needn't reach their ends.
Inputs may be any that keep to these rules, and one draw needn't show every extreme that they name: `partners_leaf`: A slot's partner leaf lies on a device (partner // 2) at most 6 away from the row leaf's device in the joint row-col order; distance 6 occurs. `partners_mid`: A slot's partner level-1 cluster index differs from the row cluster's by at most 6; distance 6 occurs. `counts_leaf`: some leaf has all 112 slots live. `counts_mid`: some level-1 cluster has all 112 slots live.
All inputs are finite; a program needn't handle non-finite values.
Results may differ from the reference program's by a relative error of at most 0.009.
Values sent between devices are 32-bit elements; how exact they have to be, the bound alone decides.
A program may use at most 192 MiB of HBM per device.

```python
import jax
import jax.numpy as jnp
from jax import lax

K = 128
NPT = 2048
LEAF_DEV = 2
LIST = 112
SPAN = 6
BANDS = 8
COLS = 4
PAIRS = 2
MID = 32
LEAVES = 64


def partner_draw(key, clusters, per_device):
    key_offset, key_slot = jax.random.split(key)
    device = jnp.arange(clusters) // per_device
    offset = jax.random.randint(key_offset, (clusters, LIST), -SPAN, SPAN + 1)
    offset = offset.at[0, 0].set(SPAN)
    target = jnp.clip(device[:, None] + offset, 0, MID - 1)
    slot = jax.random.randint(key_slot, (clusters, LIST), 0, per_device)
    return (target * per_device + slot).astype(jnp.int32)


def count_draw(key, clusters):
    key_count, key_full = jax.random.split(key)
    counts = jax.random.randint(key_count, (clusters,), 1, LIST + 1)
    full = jax.random.randint(key_full, (), 0, clusters)
    return counts.at[full].set(LIST).astype(jnp.int32)


def draw_partners_leaf(key, part):
    return partner_draw(jax.random.fold_in(key, 31), LEAVES, LEAF_DEV)


def draw_partners_mid(key, part):
    return partner_draw(jax.random.fold_in(key, 37), MID, 1)


def draw_counts_leaf(key, part):
    return count_draw(jax.random.fold_in(key, 41), LEAVES)


def draw_counts_mid(key, part):
    return count_draw(jax.random.fold_in(key, 43), MID)


def touch_ends(array, key, low, largest):
    spot = [jax.random.randint(jax.random.fold_in(key, axis), (), 0, length) for axis, length in enumerate(array.shape)]
    widest = array.shape.index(max(array.shape))
    beside = spot[:widest] + [(spot[widest] + 1) % array.shape[widest]] + spot[widest + 1:]
    return array.at[tuple(spot)].set(low).at[tuple(beside)].set(largest)


def steps_of(key, shape, pieces, low, top_value):
    factor_of, own = 1.0, jax.random.fold_in(key, 6)
    for position, shards_of in pieces:
        steps = jnp.exp(jax.random.uniform(jax.random.fold_in(own, position), (shards_of,), jnp.float32, low / len(pieces), top_value / len(pieces)))
        factor_of = factor_of * jnp.repeat(steps, shape[position] // shards_of).reshape([-1 if axis == position else 1 for axis in range(len(shape))])
    return factor_of


def gaussian(stream_key, extent, width, most, shards=(), held_as=jnp.bfloat16):
    drawn = width * jax.random.normal(stream_key, extent, jnp.float32)
    if shards:
        drawn = drawn * steps_of(stream_key, extent, shards, -0.22, 0.18)
    return jnp.clip(drawn, -most, most).astype(held_as)


def setup_inputs(seed: int = 0) -> dict:
    streams_of = jax.random.split(jax.random.key(seed), 12)
    return {
        "leaf_basis": gaussian(streams_of[0], (LEAVES, NPT, K), 1.0, 6.0, ((0, 32),)),
        "transfer_leaf": gaussian(streams_of[1], (LEAVES, K, K), K ** -0.5, 0.5, ((0, 32),), jnp.float32),
        "transfer_mid": gaussian(streams_of[2], (MID, K, K), K ** -0.5, 0.5, ((0, 32),), jnp.float32),
        "transfer_top": gaussian(streams_of[3], (BANDS, PAIRS, K, K), K ** -0.5, 0.5, ((0, 8),), jnp.float32),
        "coupling_leaf": gaussian(streams_of[4], (LEAVES, LIST, K, K), 1.0, 6.0, ((0, 32),)),
        "coupling_mid": gaussian(streams_of[5], (MID, LIST, K, K), 1.0, 6.0, ((0, 32),)),
        "partners_leaf": draw_partners_leaf(jax.random.fold_in(streams_of[11], 71), 0),
        "partners_mid": draw_partners_mid(jax.random.fold_in(streams_of[11], 71), 0),
        "counts_leaf": draw_counts_leaf(jax.random.fold_in(streams_of[11], 71), 0),
        "counts_mid": draw_counts_mid(jax.random.fold_in(streams_of[11], 71), 0),
        "ranks": touch_ends(jax.random.randint(streams_of[10], (4,), K // 2, K + 1), jax.random.fold_in(streams_of[10], 1), K // 2, K).astype(jnp.int32),
    }


HIGHEST = lax.Precision.HIGHEST

def matmul_hi(left, right):
    return jnp.matmul(left, right, precision=HIGHEST)

def flipped(matrix):
    return jnp.swapaxes(matrix, -1, -2)

def sandwich(inner, outer):
    return matmul_hi(flipped(outer), matmul_hi(inner, outer))

def right_solve(matrix, lower_factor):
    return flipped(jax.scipy.linalg.solve_triangular(lower_factor, flipped(matrix), lower=True))

def rank_mask(count, order_k):
    return (jnp.arange(order_k) < count).astype(jnp.float32)

def transform_couplings(factors_rows, blocks, partners, counts, source, mask):
    slot_ids = jnp.arange(blocks.shape[1])

    def one_cluster(packed):
        factor, block, partner, count = packed
        picked = jnp.take(source, partner, axis=0)
        left = matmul_hi(flipped(factor)[None], block.astype(jnp.float32))
        result = matmul_hi(left, picked)
        live = (slot_ids < count).astype(jnp.float32)
        return (result * live[:, None, None] * mask[:, None] * mask[None, :]).astype(jnp.bfloat16)
    return lax.map(one_cluster, (factors_rows, blocks, partners, counts))

def reference(leaf_basis, transfer_leaf, transfer_mid, transfer_top, coupling_leaf, coupling_mid, partners_leaf, partners_mid, counts_leaf, counts_mid, ranks):
    basis = leaf_basis.astype(jnp.float32)
    gram_leaf = jnp.einsum('lpi,lpj->lij', basis, basis, precision=HIGHEST) / NPT
    factor_leaf = jnp.linalg.cholesky(gram_leaf)
    gram_mid = jnp.sum(sandwich(gram_leaf, transfer_leaf).reshape(-1, LEAF_DEV, K, K), axis=1)
    factor_mid = jnp.linalg.cholesky(gram_mid)
    gram_pair = jnp.sum(sandwich(gram_mid, transfer_mid).reshape(-1, 2, K, K), axis=1)
    factor_pair = jnp.linalg.cholesky(gram_pair)
    top_flat = transfer_top.reshape(-1, K, K)
    gram_quad = jnp.sum(sandwich(gram_pair, top_flat).reshape(-1, 2, K, K), axis=1)
    factor_quad = jnp.linalg.cholesky(gram_quad)
    masks = [rank_mask(ranks[level], K) for level in range(4)]
    leaf_q = (flipped(jax.scipy.linalg.solve_triangular(factor_leaf, flipped(basis), lower=True)) * masks[0]).astype(jnp.bfloat16)
    leaf_out = right_solve(matmul_hi(flipped(factor_leaf), transfer_leaf), jnp.repeat(factor_mid, LEAF_DEV, axis=0))
    leaf_out = leaf_out * masks[0][:, None] * masks[1][None, :]
    mid_out = right_solve(matmul_hi(flipped(factor_mid), transfer_mid), jnp.repeat(factor_pair, 2, axis=0))
    mid_out = mid_out * masks[1][:, None] * masks[2][None, :]
    top_full = right_solve(matmul_hi(flipped(factor_pair), top_flat), jnp.repeat(factor_quad, 2, axis=0))
    top_full = top_full * masks[2][:, None] * masks[3][None, :]
    top_out = top_full.reshape(BANDS, COLS, K // 2, K)
    coupling_leaf_out = transform_couplings(factor_leaf, coupling_leaf, partners_leaf, counts_leaf, factor_leaf, masks[0])
    coupling_mid_out = transform_couplings(factor_mid, coupling_mid, partners_mid, counts_mid, factor_mid, masks[1])
    return (leaf_q, leaf_out, mid_out, top_out, coupling_leaf_out, coupling_mid_out)
```

```python
import functools

import jax
import jax.numpy as jnp
from jax import lax
from jax.experimental import pallas as pl
from jax.experimental.pallas import tpu as pltpu
from jax.sharding import PartitionSpec as P

SPAN = 6
PANEL = 8
GROUPS = 4
CHUNK = 16
HIGHEST = lax.Precision.HIGHEST
F32 = jnp.float32
BF16 = jnp.bfloat16
MESH = pl.DeviceIdType.MESH
LIMIT = 48 * 1024 * 1024


def dot(left, right, contract, precision=None):
    return lax.dot_general(
        left, right, (contract, ((), ())), precision=precision, preferred_element_type=F32
    )


def sandwich(inner, outer):
    inner_outer = dot(inner, outer, ((1,), (0,)), HIGHEST)
    return dot(outer, inner_outer, ((0,), (0,)), HIGHEST)


def gram_kernel(basis, t_leaf, t_mid, t_top, grams, sent, landed, send_sem, recv_sem):
    leaf_count, points = basis.shape[0], basis.shape[1]
    row, col = lax.axis_index("row"), lax.axis_index("col")
    pair = lax.div(col, 2)
    siblings = (
        col + 1 - 2 * lax.rem(col, 2),
        col + 2 - 4 * lax.rem(pair, 2),
    )
    barrier = pltpu.get_barrier_semaphore()
    for other in siblings:
        pl.semaphore_signal(barrier, inc=1, device_id=(row, other), device_id_type=MESH)
    gram_mid = None
    for leaf in range(leaf_count):
        gram = dot(basis[leaf], basis[leaf], ((0,), (0,))) / points
        grams[leaf] = gram
        term = sandwich(gram, t_leaf[leaf])
        gram_mid = term if gram_mid is None else gram_mid + term
    grams[leaf_count] = gram_mid
    pl.semaphore_wait(barrier, 2)
    outer = t_mid[0]
    inner = gram_mid
    for level in range(2):
        term = sandwich(inner, outer)
        sent[level] = term
        copy = pltpu.make_async_remote_copy(
            src_ref=sent.at[level],
            dst_ref=landed.at[level],
            send_sem=send_sem.at[level],
            recv_sem=recv_sem.at[level],
            device_id=(row, siblings[level]),
            device_id_type=MESH,
        )
        copy.start()
        copy.wait()
        inner = term + landed[level]
        grams[leaf_count + 1 + level] = inner
        outer = t_top[0, pair]


def three_parts(value):
    high = value.astype(BF16).astype(F32)
    rest = value - high
    middle = rest.astype(BF16).astype(F32)
    low = rest - middle
    return high, middle, low


def eliminate(work, order):
    batch = work.shape[0]
    rows_in = lax.broadcasted_iota(jnp.int32, (PANEL, 2 * order), 0)
    lanes = lax.broadcasted_iota(jnp.int32, (PANEL, 2 * order), 1)
    narrow = lax.broadcasted_iota(jnp.int32, (PANEL, order), 0)
    lanes_narrow = lax.broadcasted_iota(jnp.int32, (PANEL, order), 1)

    def panel(index, first_row):
        base = pl.multiple_of(index * PANEL, PANEL)
        for b in range(batch):
            wide = work[b, pl.ds(base, PANEL), :]
            turned = pltpu.roll(wide[:, :order], order - base, 1)
            columns = [
                jnp.broadcast_to(turned[:, r : r + 1], (PANEL, order)) for r in range(PANEL)
            ]
            for r in range(PANEL):
                scale = lax.rsqrt(columns[r][r : r + 1, :])
                coefficient = columns[r] * scale
                scale_wide = jnp.concatenate([scale, scale], axis=1)
                coefficient_wide = jnp.concatenate([coefficient, coefficient], axis=1)
                pivot_row = wide[r : r + 1, :] * scale_wide
                wide = jnp.where(
                    rows_in > r,
                    wide - coefficient_wide * pivot_row,
                    jnp.where(rows_in == r, pivot_row, wide),
                )
                for q in range(r + 1, PANEL):
                    columns[q] = jnp.where(
                        narrow > r,
                        columns[q] - coefficient * (columns[q][r : r + 1, :] * scale),
                        columns[q],
                    )
            wide = jnp.where((lanes >= order) | (lanes >= base + rows_in), wide, 0.0)
            work[b, pl.ds(base, PANEL), :] = wide
            after = jnp.where(lanes_narrow >= base + PANEL, wide[:, :order], 0.0)
            lh, lm, ll = three_parts(after)
            rh, rm, rl = three_parts(wide)
            left = jnp.concatenate([lh, lh, lm, lh, ll, lm], axis=0).astype(BF16)
            right = jnp.concatenate([rh, rm, rh, rl, rh, rm], axis=0).astype(BF16)
            change = dot(left[:, first_row:], right, ((0,), (0,)))
            work[b, first_row:, :] = work[b, first_row:, :] - change

    panels = order // PANEL
    for group in range(GROUPS):
        first = group * panels // GROUPS
        last = (group + 1) * panels // GROUPS

        def body(index, carry):
            panel(index, first * PANEL)
            return carry

        lax.fori_loop(first, last, body, 0)


def tree_kernel(ranks, grams, basis, t_leaf, t_mid, t_top, leaf_q, leaf_out, mid_out, top_out, packed, own, work):
    leaf_count = basis.shape[0]
    order = grams.shape[1]
    half = order // 2
    row_id = lax.broadcasted_iota(jnp.int32, (order, order), 0)
    col_id = lax.broadcasted_iota(jnp.int32, (order, order), 1)
    identity = jnp.where(row_id == col_id, 1.0, 0.0).astype(F32)
    for b in range(grams.shape[0]):
        work[b, :, :order] = grams[b]
        work[b, :, order:] = identity
    eliminate(work, order)
    pair = lax.div(lax.axis_index("col"), 2)
    mid, above, quad = leaf_count, leaf_count + 1, leaf_count + 2

    def factor(b, level):
        return jnp.where(row_id < ranks[level], work[b, :, :order], 0.0)

    def inverse(b, level):
        return jnp.where(row_id < ranks[level], work[b, :, order:], 0.0)

    def moved(b, level, transfer, parent, parent_level):
        left = dot(factor(b, level), transfer, ((1,), (0,)), HIGHEST)
        return dot(left, inverse(parent, parent_level), ((1,), (1,)), HIGHEST)

    for leaf in range(leaf_count):
        weights = inverse(leaf, 0).astype(BF16)
        leaf_q[leaf] = dot(basis[leaf], weights, ((1,), (1,))).astype(BF16)
        leaf_out[leaf] = moved(leaf, 0, t_leaf[leaf], mid, 1)
    mid_out[0] = moved(mid, 1, t_mid[0], above, 2)
    top_out[...] = moved(above, 2, t_top[0, pair], quad, 3)
    first, second, third = factor(0, 0), factor(1, 0), factor(mid, 1)
    own[0] = first.astype(BF16)
    own[1] = second.astype(BF16)
    own[2] = third.astype(BF16)
    packed[:order, :] = jnp.where(col_id >= row_id, first, second.T)
    packed[order : order + half, :] = jnp.where(
        (col_id >= row_id)[:half], third[:half], shifted_transpose(third, half)
    )
    second_diagonal = jnp.sum(jnp.where(row_id == col_id, second, 0.0), axis=0, keepdims=True)
    third_diagonal = jnp.sum(jnp.where(row_id == col_id, third, 0.0), axis=0, keepdims=True)
    packed[order + half : order + half + 8, :] = jnp.broadcast_to(second_diagonal, (8, order))
    packed[order + half + 8 : order + half + 16, :] = jnp.broadcast_to(third_diagonal, (8, order))


def shifted_transpose(matrix, half):
    return pltpu.roll(matrix.T[half:], half, 1)


def exchange_kernel(devices, columns, packed, own, table, landed, send_sem, recv_sem):
    order = own.shape[1]
    half = order // 2
    here = lax.axis_index("row") * columns + lax.axis_index("col")
    barrier = pltpu.get_barrier_semaphore()
    offsets = [sign * away for away in range(1, SPAN + 1) for sign in (1, -1)]

    def place(index):
        return (lax.div(index, columns), lax.rem(index, columns))

    def inside(index):
        return (index >= 0) & (index < devices)

    for offset in offsets:
        @pl.when(inside(here + offset))
        def _():
            pl.semaphore_signal(barrier, inc=1, device_id=place(here + offset), device_id_type=MESH)
    peers = jnp.minimum(here, SPAN) + jnp.minimum(devices - 1 - here, SPAN)
    pl.semaphore_wait(barrier, peers)

    def copy_to(offset):
        slot = SPAN - offset
        return pltpu.make_async_remote_copy(
            src_ref=packed,
            dst_ref=landed.at[slot],
            send_sem=send_sem.at[slot],
            recv_sem=recv_sem.at[slot],
            device_id=place(here + offset),
            device_id_type=MESH,
        )

    for offset in reversed(offsets):
        @pl.when(inside(here + offset))
        def _():
            copy_to(offset).start()
    for k in range(3):
        table[3 * SPAN + k] = own[k]
    row_id = lax.broadcasted_iota(jnp.int32, (order, order), 0)
    col_id = lax.broadcasted_iota(jnp.int32, (order, order), 1)
    for offset in offsets:
        slot = SPAN + offset

        @pl.when(inside(here + offset))
        def _():
            copy_to(-offset).wait_recv()
            both = landed[slot, :order, :]
            upper = jnp.where(col_id >= row_id, both, 0.0)
            lower = jnp.where(
                col_id == row_id,
                landed[slot, order + half : order + half + 1, :],
                jnp.where(col_id < row_id, both, 0.0),
            )
            table[3 * slot] = upper.astype(BF16)
            table[3 * slot + 1] = lower.T.astype(BF16)
            folded = landed[slot, order : order + half, :]
            rows = row_id[:half]
            lanes = col_id[:half]
            table[3 * slot + 2, :half, :] = jnp.where(lanes >= rows, folded, 0.0).astype(BF16)
            corner = jnp.where(lanes < rows, folded, 0.0)
            corner = jnp.concatenate([corner, jnp.zeros_like(corner)], axis=0).T
            corner = pltpu.roll(corner[:half], half, 1)
            corner = jnp.where(
                lanes == rows + half, landed[slot, order + half + 8 : order + half + 9, :], corner
            )
            table[3 * slot + 2, half:, :] = corner.astype(BF16)

    for offset in offsets:
        @pl.when(inside(here + offset))
        def _():
            copy_to(offset).wait_send()


def coupling_kernel(own_first, counts, rows, blocks, table, out):
    cluster, part = pl.program_id(0), pl.program_id(1)
    count = counts[cluster]
    mine = table[3 * SPAN + own_first + cluster]
    start = part * CHUNK
    step = 4

    for sub in range(0, CHUNK, step):
        slots = range(sub, sub + step)

        @pl.when(start + sub < count)
        def _():
            lefts = [
                dot(mine, jnp.concatenate([blocks[0, s], blocks[0, s + 1]], axis=1), ((1,), (0,)))
                .astype(BF16)
                for s in slots[::2]
            ]
            order = mine.shape[0]
            for s in slots:
                left = lefts[(s - sub) // 2][:, (s - sub) % 2 * order : ((s - sub) % 2 + 1) * order]
                result = dot(left, table[rows[cluster, start + s]], ((1,), (1,)))
                out[0, s] = jnp.where(start + s < count, result, 0.0).astype(BF16)

        @pl.when(start + sub >= count)
        def _():
            out[0, sub : sub + step] = jnp.zeros((step,) + out.shape[2:], BF16)


def transform(blocks, table, rows, counts, own_first):
    clusters, slots, order, _ = blocks.shape
    parts = slots // CHUNK

    def fetched(c, p, counts, rows):
        return (c, jnp.minimum(p, lax.div(counts[c] - 1, CHUNK)), 0, 0)

    return pl.pallas_call(
        functools.partial(coupling_kernel, own_first),
        grid_spec=pltpu.PrefetchScalarGridSpec(
            num_scalar_prefetch=2,
            grid=(clusters, parts),
            in_specs=[
                pl.BlockSpec((1, CHUNK, order, order), fetched),
                pl.BlockSpec(memory_space=pltpu.VMEM),
            ],
            out_specs=pl.BlockSpec((1, CHUNK, order, order), lambda c, p, counts, rows: (c, p, 0, 0)),
        ),
        out_shape=jax.ShapeDtypeStruct(blocks.shape, BF16),
        compiler_params=pltpu.CompilerParams(vmem_limit_bytes=LIMIT),
        name="couplings",
    )(counts, rows, blocks, table)


def on_device(
    devices,
    columns,
    leaf_basis,
    transfer_leaf,
    transfer_mid,
    transfer_top,
    coupling_leaf,
    coupling_mid,
    partners_leaf,
    partners_mid,
    counts_leaf,
    counts_mid,
    ranks,
):
    leaf_count, points, order = leaf_basis.shape
    half = order // 2
    levels = leaf_count + 3
    vmem = pl.BlockSpec(memory_space=pltpu.VMEM)
    smem = pl.BlockSpec(memory_space=pltpu.SMEM)
    grams = pl.pallas_call(
        gram_kernel,
        out_shape=jax.ShapeDtypeStruct((levels, order, order), F32),
        in_specs=[vmem] * 4,
        out_specs=vmem,
        scratch_shapes=[
            pltpu.VMEM((2, order, order), F32),
            pltpu.VMEM((2, order, order), F32),
            pltpu.SemaphoreType.DMA((2,)),
            pltpu.SemaphoreType.DMA((2,)),
        ],
        compiler_params=pltpu.CompilerParams(
            collective_id=0, has_side_effects=True, vmem_limit_bytes=LIMIT
        ),
        name="grams",
    )(leaf_basis, transfer_leaf, transfer_mid, transfer_top)
    packed_rows = order + half + 16
    leaf_q, leaf_out, mid_out, top_full, packed, own = pl.pallas_call(
        tree_kernel,
        out_shape=(
            jax.ShapeDtypeStruct(leaf_basis.shape, BF16),
            jax.ShapeDtypeStruct(transfer_leaf.shape, F32),
            jax.ShapeDtypeStruct(transfer_mid.shape, F32),
            jax.ShapeDtypeStruct((order, order), F32),
            jax.ShapeDtypeStruct((packed_rows, order), F32),
            jax.ShapeDtypeStruct((3, order, order), BF16),
        ),
        in_specs=[smem] + [vmem] * 5,
        out_specs=[vmem] * 6,
        scratch_shapes=[pltpu.VMEM((levels, order, 2 * order), F32)],
        compiler_params=pltpu.CompilerParams(vmem_limit_bytes=LIMIT),
        name="tree",
    )(ranks, grams, leaf_basis, transfer_leaf, transfer_mid, transfer_top)
    sources = 2 * SPAN + 1
    table = pl.pallas_call(
        functools.partial(exchange_kernel, devices, columns),
        out_shape=jax.ShapeDtypeStruct((3 * sources, order, order), BF16),
        in_specs=[vmem] * 2,
        out_specs=vmem,
        scratch_shapes=[
            pltpu.VMEM((sources, packed_rows, order), F32),
            pltpu.SemaphoreType.DMA((sources,)),
            pltpu.SemaphoreType.DMA((sources,)),
        ],
        compiler_params=pltpu.CompilerParams(
            collective_id=1, has_side_effects=True, vmem_limit_bytes=LIMIT
        ),
        name="exchange",
    )(packed, own)
    col_index = lax.axis_index("col")
    base = SPAN - (lax.axis_index("row") * columns + col_index)
    leaf_rows = (partners_leaf // leaf_count + base) * 3 + partners_leaf % leaf_count
    mid_rows = (partners_mid + base) * 3 + 2
    top_out = lax.dynamic_slice_in_dim(top_full, col_index % 2 * half, half, 0)
    top_out = top_out.reshape(1, 1, half, order)
    coupling_leaf_out = transform(coupling_leaf, table, leaf_rows, counts_leaf, 0)
    coupling_mid_out = transform(coupling_mid, table, mid_rows, counts_mid, 2)
    return (leaf_q, leaf_out, mid_out, top_out, coupling_leaf_out, coupling_mid_out)


def solution(mesh):
    both = ("row", "col")
    in_specs = (
        P(both, None, None),
        P(both, None, None),
        P(both, None, None),
        P("row", None, None, None),
        P(both, None, None, None),
        P(both, None, None, None),
        P(both, None),
        P(both, None),
        P(both),
        P(both),
        P(),
    )
    out_specs = (
        P(both, None, None),
        P(both, None, None),
        P(both, None, None),
        P("row", "col", None, None),
        P(both, None, None, None),
        P(both, None, None, None),
    )
    columns = mesh.shape["col"]
    return jax.shard_map(
        functools.partial(on_device, mesh.shape["row"] * columns, columns),
        mesh=mesh,
        in_specs=in_specs,
        out_specs=out_specs,
        check_vma=False,
    )
```

```python
import functools

import jax
import jax.numpy as jnp
from jax import lax
from jax.experimental import pallas as pl
from jax.experimental.pallas import tpu as pltpu
from jax.sharding import PartitionSpec as P

SPAN = 6
PANEL = 8
GROUPS = 4
CHUNK = 16
HIGHEST = lax.Precision.HIGHEST
F32 = jnp.float32
BF16 = jnp.bfloat16
MESH = pl.DeviceIdType.MESH
LIMIT = 48 * 1024 * 1024


def dot(left, right, contract, precision=None):
    return lax.dot_general(
        left, right, (contract, ((), ())), precision=precision, preferred_element_type=F32
    )


def sandwich(inner, outer):
    inner_outer = dot(inner, outer, ((1,), (0,)), HIGHEST)
    return dot(outer, inner_outer, ((0,), (0,)), HIGHEST)


def gram_kernel(basis, t_leaf, t_mid, t_top, grams, sent, landed, send_sem, recv_sem):
    leaf_count, points = basis.shape[0], basis.shape[1]
    row, col = lax.axis_index("row"), lax.axis_index("col")
    pair = lax.div(col, 2)
    siblings = (
        col + 1 - 2 * lax.rem(col, 2),
        col + 2 - 4 * lax.rem(pair, 2),
    )
    barrier = pltpu.get_barrier_semaphore()
    for other in siblings:
        pl.semaphore_signal(barrier, inc=1, device_id=(row, other), device_id_type=MESH)
    gram_mid = None
    for leaf in range(leaf_count):
        gram = dot(basis[leaf], basis[leaf], ((0,), (0,))) / points
        grams[leaf] = gram
        term = sandwich(gram, t_leaf[leaf])
        gram_mid = term if gram_mid is None else gram_mid + term
    grams[leaf_count] = gram_mid
    pl.semaphore_wait(barrier, 2)
    outer = t_mid[0]
    inner = gram_mid
    for level in range(2):
        term = sandwich(inner, outer)
        sent[level] = term
        copy = pltpu.make_async_remote_copy(
            src_ref=sent.at[level],
            dst_ref=landed.at[level],
            send_sem=send_sem.at[level],
            recv_sem=recv_sem.at[level],
            device_id=(row, siblings[level]),
            device_id_type=MESH,
        )
        copy.start()
        copy.wait()
        inner = term + landed[level]
        grams[leaf_count + 1 + level] = inner
        outer = t_top[0, pair]


def three_parts(value):
    high = value.astype(BF16).astype(F32)
    rest = value - high
    middle = rest.astype(BF16).astype(F32)
    low = rest - middle
    return high, middle, low


def eliminate(work, order):
    batch = work.shape[0]
    rows_in = lax.broadcasted_iota(jnp.int32, (PANEL, 2 * order), 0)
    lanes = lax.broadcasted_iota(jnp.int32, (PANEL, 2 * order), 1)
    narrow = lax.broadcasted_iota(jnp.int32, (PANEL, order), 0)
    lanes_narrow = lax.broadcasted_iota(jnp.int32, (PANEL, order), 1)

    def panel(index, first_row):
        base = pl.multiple_of(index * PANEL, PANEL)
        wides = [work[b, pl.ds(base, PANEL), :] for b in range(batch)]
        columns = []
        for b in range(batch):
            turned = pltpu.roll(wides[b][:, :order], order - base, 1)
            columns.append(
                [jnp.broadcast_to(turned[:, r : r + 1], (PANEL, order)) for r in range(PANEL)]
            )
        for r in range(PANEL):
            scales = [lax.rsqrt(columns[b][r][r : r + 1, :]) for b in range(batch)]
            for b in range(batch):
                scale = scales[b]
                coefficient = jnp.where(narrow > r, columns[b][r] * scale, 0.0)
                for q in range(r + 1, PANEL):
                    columns[b][q] = columns[b][q] - coefficient * (
                        columns[b][q][r : r + 1, :] * scale
                    )
                scale_wide = jnp.concatenate([scale, scale], axis=1)
                coefficient_wide = jnp.concatenate([coefficient, coefficient], axis=1)
                pivot_row = wides[b][r : r + 1, :] * scale_wide
                wides[b] = jnp.where(
                    rows_in == r, pivot_row, wides[b] - coefficient_wide * pivot_row
                )
        keep = (lanes >= order) | (lanes >= base + rows_in)
        wides = [jnp.where(keep, wide, 0.0) for wide in wides]
        for b in range(batch):
            work[b, pl.ds(base, PANEL), :] = wides[b]
        changes = []
        for wide in wides:
            after = jnp.where(lanes_narrow >= base + PANEL, wide[:, :order], 0.0)
            lh, lm, ll = three_parts(after)
            rh, rm, rl = three_parts(wide)
            left = jnp.concatenate([lh, lh, lm, lh, ll, lm], axis=0).astype(BF16)
            right = jnp.concatenate([rh, rm, rh, rl, rh, rm], axis=0).astype(BF16)
            changes.append(dot(left[:, first_row:], right, ((0,), (0,))))
        for b in range(batch):
            work[b, first_row:, :] = work[b, first_row:, :] - changes[b]

    panels = order // PANEL
    for group in range(GROUPS):
        first = group * panels // GROUPS
        last = (group + 1) * panels // GROUPS

        def body(index, carry):
            panel(index, first * PANEL)
            return carry

        lax.fori_loop(first, last, body, 0)


def tree_kernel(ranks, grams, basis, t_leaf, t_mid, t_top, leaf_q, leaf_out, mid_out, top_out, packed, own, work):
    leaf_count = basis.shape[0]
    order = grams.shape[1]
    half = order // 2
    row_id = lax.broadcasted_iota(jnp.int32, (order, order), 0)
    col_id = lax.broadcasted_iota(jnp.int32, (order, order), 1)
    identity = jnp.where(row_id == col_id, 1.0, 0.0).astype(F32)
    for b in range(grams.shape[0]):
        work[b, :, :order] = grams[b]
        work[b, :, order:] = identity
    eliminate(work, order)
    pair = lax.div(lax.axis_index("col"), 2)
    mid, above, quad = leaf_count, leaf_count + 1, leaf_count + 2

    def factor(b, level):
        return jnp.where(row_id < ranks[level], work[b, :, :order], 0.0)

    def inverse(b, level):
        return jnp.where(row_id < ranks[level], work[b, :, order:], 0.0)

    def moved(b, level, transfer, parent, parent_level):
        left = dot(factor(b, level), transfer, ((1,), (0,)), HIGHEST)
        return dot(left, inverse(parent, parent_level), ((1,), (1,)), HIGHEST)

    for leaf in range(leaf_count):
        weights = inverse(leaf, 0).astype(BF16)
        leaf_q[leaf] = dot(basis[leaf], weights, ((1,), (1,))).astype(BF16)
        leaf_out[leaf] = moved(leaf, 0, t_leaf[leaf], mid, 1)
    mid_out[0] = moved(mid, 1, t_mid[0], above, 2)
    top_out[...] = moved(above, 2, t_top[0, pair], quad, 3)
    first, second, third = factor(0, 0), factor(1, 0), factor(mid, 1)
    own[0] = first.astype(BF16)
    own[1] = second.astype(BF16)
    own[2] = third.astype(BF16)
    packed[:order, :] = jnp.where(col_id >= row_id, first, second.T)
    packed[order : order + half, :] = jnp.where(
        (col_id >= row_id)[:half], third[:half], shifted_transpose(third, half)
    )
    second_diagonal = jnp.sum(jnp.where(row_id == col_id, second, 0.0), axis=0, keepdims=True)
    third_diagonal = jnp.sum(jnp.where(row_id == col_id, third, 0.0), axis=0, keepdims=True)
    packed[order + half : order + half + 8, :] = jnp.broadcast_to(second_diagonal, (8, order))
    packed[order + half + 8 : order + half + 16, :] = jnp.broadcast_to(third_diagonal, (8, order))


def shifted_transpose(matrix, half):
    return pltpu.roll(matrix.T[half:], half, 1)


def exchange_kernel(devices, columns, packed, own, table, landed, send_sem, recv_sem):
    order = own.shape[1]
    half = order // 2
    here = lax.axis_index("row") * columns + lax.axis_index("col")
    barrier = pltpu.get_barrier_semaphore()
    offsets = [sign * away for away in range(1, SPAN + 1) for sign in (1, -1)]

    def place(index):
        return (lax.div(index, columns), lax.rem(index, columns))

    def inside(index):
        return (index >= 0) & (index < devices)

    for offset in offsets:
        @pl.when(inside(here + offset))
        def _():
            pl.semaphore_signal(barrier, inc=1, device_id=place(here + offset), device_id_type=MESH)
    peers = jnp.minimum(here, SPAN) + jnp.minimum(devices - 1 - here, SPAN)
    pl.semaphore_wait(barrier, peers)

    def copy_to(offset):
        slot = SPAN - offset
        return pltpu.make_async_remote_copy(
            src_ref=packed,
            dst_ref=landed.at[slot],
            send_sem=send_sem.at[slot],
            recv_sem=recv_sem.at[slot],
            device_id=place(here + offset),
            device_id_type=MESH,
        )

    for offset in reversed(offsets):
        @pl.when(inside(here + offset))
        def _():
            copy_to(offset).start()
    for k in range(3):
        table[3 * SPAN + k] = own[k]
    row_id = lax.broadcasted_iota(jnp.int32, (order, order), 0)
    col_id = lax.broadcasted_iota(jnp.int32, (order, order), 1)
    for offset in offsets:
        slot = SPAN + offset

        @pl.when(inside(here + offset))
        def _():
            copy_to(-offset).wait_recv()
            both = landed[slot, :order, :]
            upper = jnp.where(col_id >= row_id, both, 0.0)
            lower = jnp.where(
                col_id == row_id,
                landed[slot, order + half : order + half + 1, :],
                jnp.where(col_id < row_id, both, 0.0),
            )
            table[3 * slot] = upper.astype(BF16)
            table[3 * slot + 1] = lower.T.astype(BF16)
            folded = landed[slot, order : order + half, :]
            rows = row_id[:half]
            lanes = col_id[:half]
            table[3 * slot + 2, :half, :] = jnp.where(lanes >= rows, folded, 0.0).astype(BF16)
            corner = jnp.where(lanes < rows, folded, 0.0)
            corner = jnp.concatenate([corner, jnp.zeros_like(corner)], axis=0).T
            corner = pltpu.roll(corner[:half], half, 1)
            corner = jnp.where(
                lanes == rows + half, landed[slot, order + half + 8 : order + half + 9, :], corner
            )
            table[3 * slot + 2, half:, :] = corner.astype(BF16)

    for offset in offsets:
        @pl.when(inside(here + offset))
        def _():
            copy_to(offset).wait_send()


def coupling_kernel(own_first, counts, rows, blocks, table, out):
    cluster, part = pl.program_id(0), pl.program_id(1)
    count = counts[cluster]
    mine = table[3 * SPAN + own_first + cluster]
    start = part * CHUNK
    step = CHUNK

    for sub in range(0, CHUNK, step):
        slots = range(sub, sub + step)

        @pl.when(start + sub < count)
        def _():
            lefts = [
                dot(mine, jnp.concatenate([blocks[0, s], blocks[0, s + 1]], axis=1), ((1,), (0,)))
                .astype(BF16)
                for s in slots[::2]
            ]
            order = mine.shape[0]
            for s in slots:
                left = lefts[(s - sub) // 2][:, (s - sub) % 2 * order : ((s - sub) % 2 + 1) * order]
                result = dot(left, table[rows[cluster, start + s]], ((1,), (1,)))
                out[0, s] = jnp.where(start + s < count, result, 0.0).astype(BF16)

        @pl.when(start + sub >= count)
        def _():
            out[0, sub : sub + step] = jnp.zeros((step,) + out.shape[2:], BF16)


def transform(blocks, table, rows, counts, own_first):
    clusters, slots, order, _ = blocks.shape
    parts = slots // CHUNK

    def fetched(c, p, counts, rows):
        return (c, jnp.minimum(p, lax.div(counts[c] - 1, CHUNK)), 0, 0)

    return pl.pallas_call(
        functools.partial(coupling_kernel, own_first),
        grid_spec=pltpu.PrefetchScalarGridSpec(
            num_scalar_prefetch=2,
            grid=(clusters, parts),
            in_specs=[
                pl.BlockSpec((1, CHUNK, order, order), fetched),
                pl.BlockSpec(memory_space=pltpu.VMEM),
            ],
            out_specs=pl.BlockSpec((1, CHUNK, order, order), lambda c, p, counts, rows: (c, p, 0, 0)),
        ),
        out_shape=jax.ShapeDtypeStruct(blocks.shape, BF16),
        compiler_params=pltpu.CompilerParams(vmem_limit_bytes=LIMIT),
        name="couplings",
    )(counts, rows, blocks, table)


def on_device(
    devices,
    columns,
    leaf_basis,
    transfer_leaf,
    transfer_mid,
    transfer_top,
    coupling_leaf,
    coupling_mid,
    partners_leaf,
    partners_mid,
    counts_leaf,
    counts_mid,
    ranks,
):
    leaf_count, points, order = leaf_basis.shape
    half = order // 2
    levels = leaf_count + 3
    vmem = pl.BlockSpec(memory_space=pltpu.VMEM)
    smem = pl.BlockSpec(memory_space=pltpu.SMEM)
    grams = pl.pallas_call(
        gram_kernel,
        out_shape=jax.ShapeDtypeStruct((levels, order, order), F32),
        in_specs=[vmem] * 4,
        out_specs=vmem,
        scratch_shapes=[
            pltpu.VMEM((2, order, order), F32),
            pltpu.VMEM((2, order, order), F32),
            pltpu.SemaphoreType.DMA((2,)),
            pltpu.SemaphoreType.DMA((2,)),
        ],
        compiler_params=pltpu.CompilerParams(
            collective_id=0, has_side_effects=True, vmem_limit_bytes=LIMIT
        ),
        name="grams",
    )(leaf_basis, transfer_leaf, transfer_mid, transfer_top)
    packed_rows = order + half + 16
    leaf_q, leaf_out, mid_out, top_full, packed, own = pl.pallas_call(
        tree_kernel,
        out_shape=(
            jax.ShapeDtypeStruct(leaf_basis.shape, BF16),
            jax.ShapeDtypeStruct(transfer_leaf.shape, F32),
            jax.ShapeDtypeStruct(transfer_mid.shape, F32),
            jax.ShapeDtypeStruct((order, order), F32),
            jax.ShapeDtypeStruct((packed_rows, order), F32),
            jax.ShapeDtypeStruct((3, order, order), BF16),
        ),
        in_specs=[smem] + [vmem] * 5,
        out_specs=[vmem] * 6,
        scratch_shapes=[pltpu.VMEM((levels, order, 2 * order), F32)],
        compiler_params=pltpu.CompilerParams(vmem_limit_bytes=LIMIT),
        name="tree",
    )(ranks, grams, leaf_basis, transfer_leaf, transfer_mid, transfer_top)
    sources = 2 * SPAN + 1
    table = pl.pallas_call(
        functools.partial(exchange_kernel, devices, columns),
        out_shape=jax.ShapeDtypeStruct((3 * sources, order, order), BF16),
        in_specs=[vmem] * 2,
        out_specs=vmem,
        scratch_shapes=[
            pltpu.VMEM((sources, packed_rows, order), F32),
            pltpu.SemaphoreType.DMA((sources,)),
            pltpu.SemaphoreType.DMA((sources,)),
        ],
        compiler_params=pltpu.CompilerParams(
            collective_id=1, has_side_effects=True, vmem_limit_bytes=LIMIT
        ),
        name="exchange",
    )(packed, own)
    col_index = lax.axis_index("col")
    base = SPAN - (lax.axis_index("row") * columns + col_index)
    leaf_rows = (partners_leaf // leaf_count + base) * 3 + partners_leaf % leaf_count
    mid_rows = (partners_mid + base) * 3 + 2
    top_out = lax.dynamic_slice_in_dim(top_full, col_index % 2 * half, half, 0)
    top_out = top_out.reshape(1, 1, half, order)
    coupling_leaf_out = transform(coupling_leaf, table, leaf_rows, counts_leaf, 0)
    coupling_mid_out = transform(coupling_mid, table, mid_rows, counts_mid, 2)
    return (leaf_q, leaf_out, mid_out, top_out, coupling_leaf_out, coupling_mid_out)


def solution(mesh):
    both = ("row", "col")
    in_specs = (
        P(both, None, None),
        P(both, None, None),
        P(both, None, None),
        P("row", None, None, None),
        P(both, None, None, None),
        P(both, None, None, None),
        P(both, None),
        P(both, None),
        P(both),
        P(both),
        P(),
    )
    out_specs = (
        P(both, None, None),
        P(both, None, None),
        P(both, None, None),
        P("row", "col", None, None),
        P(both, None, None, None),
        P(both, None, None, None),
    )
    columns = mesh.shape["col"]
    return jax.shard_map(
        functools.partial(on_device, mesh.shape["row"] * columns, columns),
        mesh=mesh,
        in_specs=in_specs,
        out_specs=out_specs,
        check_vma=False,
    )
```

```python
import functools

import jax
import jax.numpy as jnp
from jax import lax
from jax.experimental import pallas as pl
from jax.experimental.pallas import tpu as pltpu
from jax.sharding import PartitionSpec as P

SPAN = 6
PANEL = 8
GROUPS = 4
CHUNK = 16
HIGHEST = lax.Precision.HIGHEST
F32 = jnp.float32
BF16 = jnp.bfloat16
MESH = pl.DeviceIdType.MESH
LIMIT = 48 * 1024 * 1024


def dot(left, right, contract, precision=None):
    return lax.dot_general(
        left, right, (contract, ((), ())), precision=precision, preferred_element_type=F32
    )


def sandwich(inner, outer):
    inner_outer = dot(inner, outer, ((1,), (0,)), HIGHEST)
    return dot(outer, inner_outer, ((0,), (0,)), HIGHEST)


def gram_kernel(basis, t_leaf, t_mid, t_top, grams, sent, landed, send_sem, recv_sem):
    leaf_count, points = basis.shape[0], basis.shape[1]
    row, col = lax.axis_index("row"), lax.axis_index("col")
    pair = lax.div(col, 2)
    siblings = (
        col + 1 - 2 * lax.rem(col, 2),
        col + 2 - 4 * lax.rem(pair, 2),
    )
    barrier = pltpu.get_barrier_semaphore()
    for other in siblings:
        pl.semaphore_signal(barrier, inc=1, device_id=(row, other), device_id_type=MESH)
    gram_mid = None
    for leaf in range(leaf_count):
        gram = dot(basis[leaf], basis[leaf], ((0,), (0,))) / points
        grams[leaf] = gram
        term = sandwich(gram, t_leaf[leaf])
        gram_mid = term if gram_mid is None else gram_mid + term
    grams[leaf_count] = gram_mid
    pl.semaphore_wait(barrier, 2)
    outer = t_mid[0]
    inner = gram_mid
    for level in range(2):
        term = sandwich(inner, outer)
        sent[level] = term
        copy = pltpu.make_async_remote_copy(
            src_ref=sent.at[level],
            dst_ref=landed.at[level],
            send_sem=send_sem.at[level],
            recv_sem=recv_sem.at[level],
            device_id=(row, siblings[level]),
            device_id_type=MESH,
        )
        copy.start()
        copy.wait()
        inner = term + landed[level]
        grams[leaf_count + 1 + level] = inner
        outer = t_top[0, pair]


def three_parts(value):
    high = value.astype(BF16).astype(F32)
    rest = value - high
    middle = rest.astype(BF16).astype(F32)
    low = rest - middle
    return high, middle, low


def eliminate(work, order):
    batch = work.shape[0]
    rows_in = lax.broadcasted_iota(jnp.int32, (PANEL, 2 * order), 0)
    lanes = lax.broadcasted_iota(jnp.int32, (PANEL, 2 * order), 1)
    narrow = lax.broadcasted_iota(jnp.int32, (PANEL, order), 0)
    lanes_narrow = lax.broadcasted_iota(jnp.int32, (PANEL, order), 1)

    def panel(index, first_row):
        base = pl.multiple_of(index * PANEL, PANEL)
        wides = [work[b, pl.ds(base, PANEL), :] for b in range(batch)]
        columns = []
        for b in range(batch):
            turned = pltpu.roll(wides[b][:, :order], order - base, 1)
            columns.append(
                [jnp.broadcast_to(turned[:, r : r + 1], (PANEL, order)) for r in range(PANEL)]
            )
        for r in range(PANEL):
            scales = [lax.rsqrt(columns[b][r][r : r + 1, :]) for b in range(batch)]
            for b in range(batch):
                scale = scales[b]
                coefficient = jnp.where(narrow > r, columns[b][r] * scale, 0.0)
                for q in range(r + 1, PANEL):
                    columns[b][q] = columns[b][q] - coefficient * (
                        columns[b][q][r : r + 1, :] * scale
                    )
                scale_wide = jnp.concatenate([scale, scale], axis=1)
                coefficient_wide = jnp.concatenate([coefficient, coefficient], axis=1)
                pivot_row = wides[b][r : r + 1, :] * scale_wide
                wides[b] = jnp.where(
                    rows_in == r, pivot_row, wides[b] - coefficient_wide * pivot_row
                )
        keep = (lanes >= order) | (lanes >= base + rows_in)
        wides = [jnp.where(keep, wide, 0.0) for wide in wides]
        for b in range(batch):
            work[b, pl.ds(base, PANEL), :] = wides[b]
        changes = []
        for wide in wides:
            after = jnp.where(lanes_narrow >= base + PANEL, wide[:, :order], 0.0)
            lh, lm, ll = three_parts(after)
            rh, rm, rl = three_parts(wide)
            left = jnp.concatenate([lh, lh, lm, lh, ll, lm], axis=0).astype(BF16)
            right = jnp.concatenate([rh, rm, rh, rl, rh, rm], axis=0).astype(BF16)
            changes.append(dot(left[:, first_row:], right, ((0,), (0,))))
        for b in range(batch):
            work[b, first_row:, :] = work[b, first_row:, :] - changes[b]

    panels = order // PANEL
    for group in range(GROUPS):
        first = group * panels // GROUPS
        last = (group + 1) * panels // GROUPS

        def body(index, carry):
            panel(index, first * PANEL)
            return carry

        lax.fori_loop(first, last, body, 0)


def tree_kernel(ranks, grams, basis, t_leaf, t_mid, t_top, leaf_q, leaf_out, mid_out, top_out, packed, own, work, top_full):
    leaf_count = basis.shape[0]
    order = grams.shape[1]
    half = order // 2
    row_id = lax.broadcasted_iota(jnp.int32, (order, order), 0)
    col_id = lax.broadcasted_iota(jnp.int32, (order, order), 1)
    identity = jnp.where(row_id == col_id, 1.0, 0.0).astype(F32)
    for b in range(grams.shape[0]):
        work[b, :, :order] = grams[b]
        work[b, :, order:] = identity
    eliminate(work, order)
    pair = lax.div(lax.axis_index("col"), 2)
    mid, above, quad = leaf_count, leaf_count + 1, leaf_count + 2

    def factor(b, level):
        return jnp.where(row_id < ranks[level], work[b, :, :order], 0.0)

    def inverse(b, level):
        return jnp.where(row_id < ranks[level], work[b, :, order:], 0.0)

    def moved(b, level, transfer, parent, parent_level):
        left = dot(factor(b, level), transfer, ((1,), (0,)), HIGHEST)
        return dot(left, inverse(parent, parent_level), ((1,), (1,)), HIGHEST)

    for leaf in range(leaf_count):
        weights = inverse(leaf, 0).astype(BF16)
        leaf_q[leaf] = dot(basis[leaf], weights, ((1,), (1,))).astype(BF16)
        leaf_out[leaf] = moved(leaf, 0, t_leaf[leaf], mid, 1)
    mid_out[0] = moved(mid, 1, t_mid[0], above, 2)
    top_full[...] = moved(above, 2, t_top[0, pair], quad, 3)
    side = lax.rem(lax.axis_index("col"), 2)
    top_out[...] = top_full[pl.ds(pl.multiple_of(side * half, half), half), :]
    first, second, third = factor(0, 0), factor(1, 0), factor(mid, 1)
    own[0] = first.astype(BF16)
    own[1] = second.astype(BF16)
    own[2] = third.astype(BF16)
    packed[:order, :] = jnp.where(col_id >= row_id, first, second.T)
    packed[order : order + half, :] = jnp.where(
        (col_id >= row_id)[:half], third[:half], shifted_transpose(third, half)
    )
    second_diagonal = jnp.sum(jnp.where(row_id == col_id, second, 0.0), axis=0, keepdims=True)
    third_diagonal = jnp.sum(jnp.where(row_id == col_id, third, 0.0), axis=0, keepdims=True)
    packed[order + half : order + half + 8, :] = jnp.broadcast_to(second_diagonal, (8, order))
    packed[order + half + 8 : order + half + 16, :] = jnp.broadcast_to(third_diagonal, (8, order))


def shifted_transpose(matrix, half):
    return pltpu.roll(matrix.T[half:], half, 1)


def exchange_kernel(devices, columns, packed, own, table, landed, send_sem, recv_sem):
    order = own.shape[1]
    half = order // 2
    leaf_count = own.shape[0] - 1
    here = lax.axis_index("row") * columns + lax.axis_index("col")
    reach = (SPAN + 1) // 2
    sources = 2 * (2 * reach + 1)
    groups = devices // 2
    group = lax.div(here, 2)
    parity = here - 2 * group
    sibling = here + 1 - 2 * parity
    barrier = pltpu.get_barrier_semaphore()
    offsets = [sign * away for away in range(1, reach + 1) for sign in (1, -1)]

    def place(index):
        return (lax.div(index, columns), lax.rem(index, columns))

    def inside(offset):
        return (group + offset >= 0) & (group + offset < groups)

    for offset in offsets:
        @pl.when(inside(offset))
        def _():
            pl.semaphore_signal(
                barrier, inc=1, device_id=place(here + 2 * offset), device_id_type=MESH
            )
    pl.semaphore_signal(barrier, inc=1, device_id=place(sibling), device_id_type=MESH)
    peers = jnp.minimum(group, reach) + jnp.minimum(groups - 1 - group, reach) + 1
    pl.semaphore_wait(barrier, peers)

    def copy(source, slot, sem, target):
        return pltpu.make_async_remote_copy(
            src_ref=source,
            dst_ref=landed.at[slot],
            send_sem=send_sem.at[sem],
            recv_sem=recv_sem.at[slot],
            device_id=place(target),
            device_id_type=MESH,
        )

    def direct(offset):
        return copy(packed, 2 * (reach - offset) + parity, reach - offset, here + 2 * offset)

    def onward(offset, side):
        slot = 2 * (reach + offset) + side
        return copy(landed.at[slot], slot, 3 * reach + 1 + offset, sibling)

    beside = copy(packed, 2 * reach + parity, reach, sibling)
    order_sent = offsets[::-1]
    for offset in order_sent:
        @pl.when(inside(offset))
        def _():
            direct(offset).start()
    beside.start()
    for k in range(leaf_count):
        table[leaf_count * (2 * reach + parity) + k] = own[k]
    table[leaf_count * sources + 2 * reach + parity] = own[leaf_count]
    row_id = lax.broadcasted_iota(jnp.int32, (order, order), 0)
    col_id = lax.broadcasted_iota(jnp.int32, (order, order), 1)

    def unpack(slot):
        both = landed[slot, :order, :]
        upper = jnp.where(col_id >= row_id, both, 0.0)
        lower = jnp.where(
            col_id == row_id,
            landed[slot, order + half : order + half + 1, :],
            jnp.where(col_id < row_id, both, 0.0),
        )
        table[leaf_count * slot] = upper.astype(BF16)
        table[leaf_count * slot + 1] = lower.T.astype(BF16)
        folded = landed[slot, order : order + half, :]
        rows = row_id[:half]
        lanes = col_id[:half]
        middle = leaf_count * sources + slot
        table[middle, :half, :] = jnp.where(lanes >= rows, folded, 0.0).astype(BF16)
        corner = jnp.where(lanes < rows, folded, 0.0)
        corner = jnp.concatenate([corner, jnp.zeros_like(corner)], axis=0).T
        corner = pltpu.roll(corner[:half], half, 1)
        corner = jnp.where(
            lanes == rows + half, landed[slot, order + half + 8 : order + half + 9, :], corner
        )
        table[middle, half:, :] = corner.astype(BF16)

    other = 1 - parity
    copy(packed, 2 * reach + other, reach, sibling).wait_recv()
    unpack(2 * reach + other)
    for offset in offsets:
        @pl.when(inside(offset))
        def _():
            direct(-offset).wait_recv()
            onward(offset, parity).start()
            unpack(2 * (reach + offset) + parity)
    for offset in offsets:
        @pl.when(inside(offset))
        def _():
            onward(offset, other).wait_recv()
            unpack(2 * (reach + offset) + other)
    for offset in offsets:
        @pl.when(inside(offset))
        def _():
            direct(offset).wait_send()
            onward(offset, parity).wait_send()
    beside.wait_send()


def coupling_kernel(own_first, leaf_count, columns, counts, partners, blocks, own, table, out):
    cluster, part = pl.program_id(0), pl.program_id(1)
    count = counts[cluster]
    mine = own[own_first + cluster]
    here = lax.axis_index("row") * columns + lax.axis_index("col")
    reach = (SPAN + 1) // 2
    base = 2 * reach - (here - lax.rem(here, 2))
    shift = leaf_count * base
    if own_first:
        shift = leaf_count * 2 * (2 * reach + 1) + base
    start = part * CHUNK
    step = CHUNK

    for sub in range(0, CHUNK, step):
        slots = range(sub, sub + step)

        @pl.when(start + sub < count)
        def _():
            lefts = [
                dot(mine, jnp.concatenate([blocks[0, s], blocks[0, s + 1]], axis=1), ((1,), (0,)))
                .astype(BF16)
                for s in slots[::2]
            ]
            order = mine.shape[0]
            for s in slots:
                left = lefts[(s - sub) // 2][:, (s - sub) % 2 * order : ((s - sub) % 2 + 1) * order]
                result = dot(left, table[partners[cluster, start + s] + shift], ((1,), (1,)))
                out[0, s] = jnp.where(start + s < count, result, 0.0).astype(BF16)

        @pl.when(start + sub >= count)
        def _():
            out[0, sub : sub + step] = jnp.zeros((step,) + out.shape[2:], BF16)


def transform(blocks, own, table, partners, counts, own_first, columns):
    clusters, slots, order, _ = blocks.shape
    parts = slots // CHUNK

    def fetched(c, p, counts, partners):
        return (c, jnp.minimum(p, lax.div(counts[c] - 1, CHUNK)), 0, 0)

    return pl.pallas_call(
        functools.partial(coupling_kernel, own_first, own.shape[0] - 1, columns),
        grid_spec=pltpu.PrefetchScalarGridSpec(
            num_scalar_prefetch=2,
            grid=(clusters, parts),
            in_specs=[
                pl.BlockSpec((1, CHUNK, order, order), fetched),
                pl.BlockSpec(memory_space=pltpu.VMEM),
                pl.BlockSpec(memory_space=pltpu.VMEM),
            ],
            out_specs=pl.BlockSpec((1, CHUNK, order, order), lambda c, p, counts, partners: (c, p, 0, 0)),
        ),
        out_shape=jax.ShapeDtypeStruct(blocks.shape, BF16),
        compiler_params=pltpu.CompilerParams(vmem_limit_bytes=LIMIT),
        name="couplings",
    )(counts, partners, blocks, own, table)


def on_device(
    devices,
    columns,
    leaf_basis,
    transfer_leaf,
    transfer_mid,
    transfer_top,
    coupling_leaf,
    coupling_mid,
    partners_leaf,
    partners_mid,
    counts_leaf,
    counts_mid,
    ranks,
):
    leaf_count, points, order = leaf_basis.shape
    half = order // 2
    levels = leaf_count + 3
    vmem = pl.BlockSpec(memory_space=pltpu.VMEM)
    smem = pl.BlockSpec(memory_space=pltpu.SMEM)
    grams = pl.pallas_call(
        gram_kernel,
        out_shape=jax.ShapeDtypeStruct((levels, order, order), F32),
        in_specs=[vmem] * 4,
        out_specs=vmem,
        scratch_shapes=[
            pltpu.VMEM((2, order, order), F32),
            pltpu.VMEM((2, order, order), F32),
            pltpu.SemaphoreType.DMA((2,)),
            pltpu.SemaphoreType.DMA((2,)),
        ],
        compiler_params=pltpu.CompilerParams(
            collective_id=0, has_side_effects=True, vmem_limit_bytes=LIMIT
        ),
        name="grams",
    )(leaf_basis, transfer_leaf, transfer_mid, transfer_top)
    packed_rows = order + half + 16
    leaf_q, leaf_out, mid_out, top_half, packed, own = pl.pallas_call(
        tree_kernel,
        out_shape=(
            jax.ShapeDtypeStruct(leaf_basis.shape, BF16),
            jax.ShapeDtypeStruct(transfer_leaf.shape, F32),
            jax.ShapeDtypeStruct(transfer_mid.shape, F32),
            jax.ShapeDtypeStruct((half, order), F32),
            jax.ShapeDtypeStruct((packed_rows, order), F32),
            jax.ShapeDtypeStruct((3, order, order), BF16),
        ),
        in_specs=[smem] + [vmem] * 5,
        out_specs=[vmem] * 6,
        scratch_shapes=[
            pltpu.VMEM((levels, order, 2 * order), F32),
            pltpu.VMEM((order, order), F32),
        ],
        compiler_params=pltpu.CompilerParams(vmem_limit_bytes=LIMIT),
        name="tree",
    )(ranks, grams, leaf_basis, transfer_leaf, transfer_mid, transfer_top)
    sources = 2 * (2 * ((SPAN + 1) // 2) + 1)
    table = pl.pallas_call(
        functools.partial(exchange_kernel, devices, columns),
        out_shape=jax.ShapeDtypeStruct((3 * sources, order, order), BF16),
        in_specs=[vmem] * 2,
        out_specs=vmem,
        scratch_shapes=[
            pltpu.VMEM((sources, packed_rows, order), F32),
            pltpu.SemaphoreType.DMA((sources,)),
            pltpu.SemaphoreType.DMA((sources,)),
        ],
        compiler_params=pltpu.CompilerParams(
            collective_id=1, has_side_effects=True, vmem_limit_bytes=LIMIT
        ),
        name="exchange",
    )(packed, own)
    top_out = top_half.reshape(1, 1, half, order)
    coupling_leaf_out = transform(
        coupling_leaf, own, table, partners_leaf, counts_leaf, 0, columns
    )
    coupling_mid_out = transform(
        coupling_mid, own, table, partners_mid, counts_mid, leaf_count, columns
    )
    return (leaf_q, leaf_out, mid_out, top_out, coupling_leaf_out, coupling_mid_out)


def solution(mesh):
    both = ("row", "col")
    in_specs = (
        P(both, None, None),
        P(both, None, None),
        P(both, None, None),
        P("row", None, None, None),
        P(both, None, None, None),
        P(both, None, None, None),
        P(both, None),
        P(both, None),
        P(both),
        P(both),
        P(),
    )
    out_specs = (
        P(both, None, None),
        P(both, None, None),
        P(both, None, None),
        P("row", "col", None, None),
        P(both, None, None, None),
        P(both, None, None, None),
    )
    columns = mesh.shape["col"]
    return jax.shard_map(
        functools.partial(on_device, mesh.shape["row"] * columns, columns),
        mesh=mesh,
        in_specs=in_specs,
        out_specs=out_specs,
        check_vma=False,
    )
```
